256 devices in a mesh: grp: 8 (over x_hi, y), mem: 32 (over x_lo, z, core).
Axes of the slice: x: 4 (x_hi: 2, x_lo: 2; x = x_hi * 2 + x_lo), y: 4, z: 8, core: 2. Of those that a mesh axis runs over, the one named last changes fastest.
Arguments:
- images: bfloat16 [32768, 1152], P(('grp', 'mem')), may hold values from -1 to 1
- texts: bfloat16 [32768, 1152], P(('grp', 'mem')), may hold values from -1 to 1
- log_temp: float32 [1], replicated, may hold values from 2.3 to 4.6
- bias: float32 [1], replicated, may hold values from -12 to -5
Outputs:
- image_grad: float32 [32768, 1152], P(('grp', 'mem'))
- text_grad: float32 [32768, 1152], P(('grp', 'mem'))
- loss: float32 [1], replicated
- bias_grad: float32 [1], replicated
The draws below stay inside these ranges and needn't reach their ends.
All inputs are finite; a program needn't handle non-finite values.
Results may differ from the reference program's by a relative error of at most 0.0038.
Values may be sent and summed in bfloat16 or wider, within the bound.
A program may use at most 128 MiB of HBM per device.

```python
import jax
import jax.numpy as jnp
from jax import lax

D = 1152
ROWS_DEV = 128
ROUNDS = 4
PAIRS = 32768
N_GRP = 8
N_MEM = 32


def pair_mix(key):
    count = max(PAIRS // 64, 4)
    center_key = jax.random.fold_in(key, 101)
    pick_key = jax.random.fold_in(key, 102)
    pair_key = jax.random.fold_in(key, 103)
    centers = jax.random.normal(center_key, (count, D), jnp.float32)
    picks = jax.random.randint(pick_key, (PAIRS,), 0, count)
    shared = jax.random.normal(pair_key, (PAIRS, D), jnp.float32)
    return 0.35 * centers[picks] + 0.55 * shared


def draw_images(key, part):
    mixed = pair_mix(key)
    key = jax.random.fold_in(key, 3)
    noise_key = jax.random.fold_in(key, 11)
    scale_key = jax.random.fold_in(key, 12)
    noise = jax.random.normal(noise_key, (PAIRS, D), jnp.float32)
    scales = jnp.exp(jax.random.uniform(scale_key, (PAIRS, 1), jnp.float32, -0.6931472, 2.0794415))
    values = mixed + 0.75 * noise
    return jnp.clip(0.02 * scales * values, -1.0, 1.0).astype(jnp.bfloat16)


def draw_texts(key, part):
    mixed = pair_mix(key)
    key = jax.random.fold_in(key, 4)
    noise_key = jax.random.fold_in(key, 21)
    scale_key = jax.random.fold_in(key, 22)
    noise = jax.random.normal(noise_key, (PAIRS, D), jnp.float32)
    scales = jnp.exp(jax.random.uniform(scale_key, (PAIRS, 1), jnp.float32, -0.6931472, 2.0794415))
    values = mixed + 0.75 * noise
    return jnp.clip(0.02 * scales * values, -1.0, 1.0).astype(jnp.bfloat16)


def setup_inputs(seed: int = 0) -> dict:
    keys = jax.random.split(jax.random.key(seed), 5)
    return {
        "images": draw_images(jax.random.fold_in(keys[4], 71), 0),
        "texts": draw_texts(jax.random.fold_in(keys[4], 71), 0),
        "log_temp": jnp.clip(jax.random.uniform(keys[2], (1,), jnp.float32, 2.3, 4.6), 2.3, 4.6),
        "bias": jnp.clip(jax.random.uniform(keys[3], (1,), jnp.float32, -12.0, -5.0), -12.0, -5.0),
    }


def normalize(values):
    full = values.astype(jnp.float32)
    inverse = lax.rsqrt(lax.optimization_barrier(jnp.sum(full * full, axis=-1, keepdims=True)) + 1e-06)
    return (full * inverse, inverse)

def reference(images, texts, log_temp, bias):
    x_unit, x_inverse = normalize(images)
    y_unit, y_inverse = normalize(texts)
    x_low = x_unit.astype(jnp.bfloat16)
    y_low = y_unit.astype(jnp.bfloat16)
    temp = jnp.exp(log_temp[0])
    offset = bias[0]
    block_rows = ROWS_DEV * N_MEM
    total = PAIRS

    def one_block(carry, index):
        loss_sum, c_sum, gy_acc = carry
        start = (index * block_rows).astype(jnp.int32)
        rows = lax.dynamic_slice_in_dim(x_low, start, block_rows, 0)
        row_ids = start + jnp.arange(block_rows, dtype=jnp.int32)
        gx_rows = jnp.zeros((block_rows, D), jnp.float32)
        for offset_step in range(ROUNDS):
            source = ((index - offset_step + N_GRP) % N_GRP).astype(jnp.int32)
            text_start = (source * block_rows).astype(jnp.int32)
            text_rows = lax.dynamic_slice_in_dim(y_low, text_start, block_rows, 0)
            text_ids = text_start + jnp.arange(block_rows, dtype=jnp.int32)
            logits = temp * jnp.dot(rows, text_rows.T, preferred_element_type=jnp.float32) + offset
            sign = jnp.where(row_ids[:, None] == text_ids[None, :], 1.0, -1.0).astype(jnp.float32)
            per = jax.nn.softplus(-sign * logits)
            weight = -sign * jax.nn.sigmoid(-sign * logits)
            weight_low = weight.astype(jnp.bfloat16)
            gx_rows = gx_rows + jnp.dot(weight_low, text_rows, preferred_element_type=jnp.float32)
            old = lax.dynamic_slice_in_dim(gy_acc, text_start, block_rows, 0)
            new = old + jnp.dot(weight_low.T, rows, preferred_element_type=jnp.float32)
            gy_acc = lax.dynamic_update_slice_in_dim(gy_acc, new, text_start, 0)
            loss_sum = loss_sum + jnp.sum(per)
            c_sum = c_sum + jnp.sum(weight)
        return ((loss_sum, c_sum, gy_acc), gx_rows)
    start_carry = (jnp.zeros((), jnp.float32), jnp.zeros((), jnp.float32), jnp.zeros((total, D), jnp.float32))
    (loss_sum, c_sum, gy_acc), gx_blocks = lax.scan(one_block, start_carry, jnp.arange(N_GRP, dtype=jnp.int32))
    gx_full = temp * gx_blocks.reshape(total, D)
    gy_full = temp * gy_acc
    image_grad = (gx_full - x_unit * lax.optimization_barrier(jnp.sum(x_unit * gx_full, axis=-1, keepdims=True))) * x_inverse
    text_grad = (gy_full - y_unit * lax.optimization_barrier(jnp.sum(y_unit * gy_full, axis=-1, keepdims=True))) * y_inverse
    count = jnp.float32(total)
    return (image_grad, text_grad, (loss_sum / count).reshape(1), (c_sum / count).reshape(1))
```

```python
import functools
import math

import jax
import jax.numpy as jnp
from jax import lax
from jax.experimental import pallas as pl
from jax.experimental.pallas import tpu as pltpu
from jax.sharding import PartitionSpec as P

MESH = pl.DeviceIdType.MESH
F32 = jnp.float32
BF16 = jnp.bfloat16
LOG2E = math.log2(math.e)
LN2 = math.log(2.0)

P_SLOT = {0: 0, 1: 2, 3: 3, 2: 5}
S_SLOT = {0: 1, 1: 4, 3: 6, 2: 7}
T_PLACE = {"R1": (0, 0), "L1": (0, 1), "R2": (1, 0), "L2": (1, 1), "R3": (2, 0), "L3": (2, 1), "R0": (3, 0), "L0": (3, 0), "R4": (3, 1), "L4": (3, 1)}


def unit_of(n):
    b = jnp.where(n < 4, n, jnp.where(n < 12, lax.rem(n, 6), jnp.where(n < 21, jnp.minimum(n - 12, 6), jnp.where(n < 28, n - 21, 7))))
    q = jnp.where(n < 6, 0, jnp.where(n < 12, 1, jnp.where(n < 18, 2, jnp.where(n < 21, n - 18, jnp.where(n < 28, 3, n - 28)))))
    return b, q


def log1p_sum(q):
    series = q * (1.0 - q * (0.5 - q * (1.0 / 3.0 - q * 0.25)))
    return jnp.where(q < 0.0078125, series, jnp.log(1.0 + q))


def kernel(
    images, texts, log_temp, bias,
    image_grad, text_grad, loss_out, bias_out,
    ibuf, tbuf, g_i, g_t, cbuf, ctbuf, shift, sums,
    tw_send, tw_recv, pt_send, pt_recv, dr_send, dr_recv, zl_send, zl_recv, zr_send, zr_recv,
    l1, l2, l3, l4, ssem, rsem,
):
    N, W = images.shape
    H = N // 2
    g = lax.axis_index("grp")
    m = lax.axis_index("mem")
    y = lax.rem(g, 4)
    xh = lax.div(g, 4)
    xl = lax.div(m, 16)
    z = lax.rem(lax.div(m, 2), 8)
    core = lax.rem(m, 2)

    def dev(grp, x_lo, zz, cc):
        return (grp, x_lo * 16 + zz * 2 + cc)

    twin = dev(g, xl, z, 1 - core)
    ring = [dev(g, xl, lax.rem(z + k, 8), core) for k in range(8)]
    ahead, back = ring[1], ring[7]
    partner = dev(g, 1 - xl, z, core)
    other = lax.rem(g + 4, 8)
    adjacent = dev(other, 1 - xl, z, core)
    far = dev(other, xl, z, core)
    dest, source = {}, {}
    for r in (1, 2, 3):
        dest[r] = dev(lax.rem(g + r + 4, 8), jnp.where(y + r < 4, 1 - xl, xl), z, core)
        source[r] = dev(lax.rem(g + 12 - r, 8), jnp.where(y - r >= 0, 1 - xl, xl), z, core)

    count = [0]
    started = []

    def message(src, dst, device):
        i = count[0]
        count[0] += 1
        return pltpu.make_async_remote_copy(
            src_ref=src, dst_ref=dst, send_sem=ssem.at[i], recv_sem=rsem.at[i], device_id=device, device_id_type=MESH
        )

    def start(*copies):
        for c in copies:
            c.start()
            started.append(c)

    def place(name, half):
        q, side = T_PLACE[name]
        return tbuf.at[q, pl.ds(side * N + half * H, H)]

    right, left = [], []
    for k in range(7):
        a, b_ = k // 2, k // 2 + 1
        right.append(message(place(f"R{a}", k % 2), place(f"R{b_}", k % 2), ahead))
        left.append(message(place(f"L{a}", 1 - k % 2), place(f"L{b_}", 1 - k % 2), back))

    def own(b):
        return ibuf.at[b, pl.ds(0, N)]

    direct = {r: message(own(0), own(P_SLOT[r]), dest[r]) for r in (1, 3, 2)}
    across = {r: message(own(P_SLOT[r]), own(S_SLOT[r]), partner) for r in (0, 1, 3, 2)}
    twins = [message(own(b), ibuf.at[b, pl.ds(N, N)], twin) for b in range(8)]
    back_twin = [message(tw_send.at[b], tw_recv.at[b], twin) for b in range(8)]
    back_across = {r: message(pt_send.at[r], pt_recv.at[r], partner) for r in range(4)}
    back_direct = {r: message(dr_send.at[r - 1], dr_recv.at[r - 1], source[r]) for r in (1, 2, 3)}
    back_left = [message(zl_send.at[k], zl_recv.at[k], back) for k in range(7)]
    back_right = [message(zr_send.at[k], zr_recv.at[k], ahead) for k in range(7)]
    x = xh * 2 + xl
    loss_twin = message(l1.at[0], l1.at[1], twin)
    loss_ring = [message(l2.at[z], l2.at[z], ring[k]) for k in range(1, 8)]
    loss_row = [message(l3.at[x], l3.at[x], d) for d in (partner, adjacent, far)]
    loss_col = [message(l4.at[y], l4.at[y], dest[r]) for r in (1, 2, 3)]

    peers = [twin, *ring[1:], partner, adjacent, far, *dest.values(), *source.values()]
    barrier = pltpu.get_barrier_semaphore()
    for p in peers:
        pl.semaphore_signal(barrier, inc=1, device_id=p, device_id_type=MESH)

    def unit_rows(ref):
        full = ref[...].astype(F32)
        inverse = lax.rsqrt(jnp.sum(full * full, axis=-1, keepdims=True) + 1e-06)
        return full * inverse, inverse

    tbuf[3, 0:N] = unit_rows(texts)[0].astype(BF16)
    ibuf[0, 0:N] = unit_rows(images)[0].astype(BF16)
    pl.semaphore_wait(barrier, len(peers))
    start(right[0], left[0], across[0], direct[1], direct[3], direct[2], right[1], left[1], twins[0])

    temp = jnp.max(jnp.exp(jnp.full((8, 128), log_temp[0], F32)))
    offset = bias[0]
    scale = temp * LOG2E
    offset2 = offset * LOG2E
    row = lax.broadcasted_iota(jnp.int32, (2 * N, 2 * N), 0)
    col = lax.broadcasted_iota(jnp.int32, (2 * N, 2 * N), 1)
    shift[0] = jnp.full((2 * N, 2 * N), offset2, F32)
    shift[1] = jnp.where((row == col) & (row < N), -1e30, offset2)
    sums[...] = jnp.zeros_like(sums)

    def clear(i, carry):
        zeros = jnp.zeros((32, W), F32)
        g_i[lax.div(i, 8), pl.ds(pl.multiple_of(lax.rem(i, 8) * 32, 32), 32)] = zeros

        @pl.when(i < 32)
        def _():
            g_t[lax.div(i, 8), pl.ds(pl.multiple_of(lax.rem(i, 8) * 32, 32), 32)] = zeros

        return carry

    lax.fori_loop(0, 64, clear, 0)

    def hop(k):
        right[k].wait_recv()
        left[k].wait_recv()
        if k + 2 < 7:
            start(right[k + 2], left[k + 2])

    def logits(b, q):
        return lax.dot_general(ibuf[b], tbuf[q], (((1,), (1,)), ((), ())), preferred_element_type=F32)

    def weights(dots, masked):
        u = dots * scale + shift[masked]
        e = jnp.exp2(-jnp.abs(u))
        d = 1.0 + e
        inv = pl.reciprocal(d, approx=True)
        inv = inv * (2.0 - d * inv)
        c = jnp.where(u >= 0.0, 1.0, e) * inv
        cb = c.astype(BF16)
        cbuf[...] = cb
        ctbuf[...] = cb.T
        parts = [e[8 * i : 8 * i + 8] for i in range(2 * N // 8)]
        while len(parts) > 1:
            parts = [a + (h + a * h) for a, h in zip(parts[::2], parts[1::2])]
        tail = log1p_sum(parts[0])
        linear = jnp.sum(jnp.maximum(u, 0.0).reshape(2 * N // 8, 8, 2 * N), axis=0)
        csum = jnp.sum(c.reshape(2 * N // 8, 8, 2 * N), axis=0)
        sums[0] += tail + linear * LN2
        sums[1] += csum

    def grads(b, q):
        c, ct = cbuf[...], ctbuf[...]
        for lo in range(0, W, 512):
            hi = min(lo + 512, W)
            g_i[b, :, lo:hi] += jnp.dot(c, tbuf[q, :, lo:hi], preferred_element_type=F32)
            g_t[q, :, lo:hi] += jnp.dot(ct, ibuf[b, :, lo:hi], preferred_element_type=F32)

    def pass_on(r):
        direct[r].wait_recv()
        start(across[r], twins[P_SLOT[r]])

    def pass_twin(r):
        across[r].wait_recv()
        start(twins[S_SLOT[r]])

    hop(0)
    hop(1)
    pass_on(1)
    pass_on(3)
    pass_twin(0)
    for b in (0, 1, 2, 3):
        twins[b].wait_recv()

    def step(n, carry):
        @pl.when(n == 4)
        def _():
            hop(2)
            hop(3)
            pass_on(2)
            pass_twin(1)
            twins[4].wait_recv()
            twins[5].wait_recv()

        @pl.when(n == 8)
        def _():
            hop(4)

        @pl.when(n == 12)
        def _():
            hop(5)

        @pl.when(n == 18)
        def _():
            pass_twin(3)
            twins[6].wait_recv()

        @pl.when(n == 21)
        def _():
            hop(6)

        @pl.when(n == 28)
        def _():
            pass_twin(2)
            twins[7].wait_recv()

        b, q = unit_of(n)
        before_b, before_q = unit_of(n - 1)
        dots = logits(b, q)
        grads(before_b, before_q)
        weights(dots, jnp.where(n == 21, 1, 0))
        return carry

    weights(logits(0, 0), 0)
    lax.fori_loop(1, 32, step, 0)
    grads(7, 3)

    def text_part(name, half):
        q, side = T_PLACE[name]
        return g_t[q, side * N + half * H : side * N + half * H + H]

    def ring_back(k):
        name = 4 - (k + 1) // 2
        for sign, send, recv, out in (("R", zl_send, zl_recv, back_left), ("L", zr_send, zr_recv, back_right)):
            half = (k % 2) if sign == "R" else 1 - (k % 2)
            share = text_part(f"{sign}{name}", half)
            if k >= 2:
                out[k - 2].wait_recv()
                share = share + recv[k - 2].astype(F32)
            send[k] = share.astype(BF16)
            start(out[k])

    ring_back(0)
    ring_back(1)
    order = [4, 6, 7, 1, 2, 3, 5, 0]
    for b in order:
        tw_send[b] = g_i[b, N : 2 * N].astype(BF16)
        start(back_twin[b])

    x_unit, x_inverse = unit_rows(images)
    y_unit, y_inverse = unit_rows(texts)
    x_low = x_unit.astype(BF16).astype(F32)
    y_low = y_unit.astype(BF16).astype(F32)
    positive = temp * jnp.sum(x_low * y_low, axis=-1, keepdims=True) + offset
    e = jnp.exp(-jnp.abs(positive))
    d = 1.0 + e
    own_c = -jnp.where(positive >= 0.0, e, 1.0) / d
    own_loss = jnp.maximum(-positive, 0.0) + log1p_sum(e)
    own_cb = own_c.astype(BF16).astype(F32)

    first = lax.broadcasted_iota(jnp.int32, (8, 128), 0) + lax.broadcasted_iota(jnp.int32, (8, 128), 1) == 0
    l1[0, 0:8] = sums[0, :, 0:128] + sums[0, :, 128:256] + jnp.where(first, jnp.sum(own_loss), 0.0)
    l1[0, 8:16] = sums[1, :, 0:128] + sums[1, :, 128:256] + jnp.where(first, jnp.sum(own_c), 0.0)
    start(loss_twin)

    def send_across(r):
        b = S_SLOT[r]
        back_twin[b].wait_recv()
        pt_send[r] = (g_i[b, 0:N] + tw_recv[b].astype(F32)).astype(BF16)
        start(back_across[r])

    def gather_across(r):
        b = P_SLOT[r]
        back_twin[b].wait_recv()
        back_across[r].wait_recv()
        return g_i[b, 0:N] + tw_recv[b].astype(F32) + pt_recv[r].astype(F32)

    def send_home(r):
        dr_send[r - 1] = gather_across(r).astype(BF16)
        start(back_direct[r])

    for r in (1, 3, 2, 0):
        send_across(r)
    loss_twin.wait_recv()
    l2[z] = l1[0] + l1[1]
    start(*loss_ring)
    ring_back(2)
    ring_back(3)
    send_home(1)
    for c in loss_ring:
        c.wait_recv()
    l3[x] = sum([l2[k] for k in range(1, 8)], l2[0])
    start(*loss_row)
    ring_back(4)
    ring_back(5)
    send_home(3)
    for c in loss_row:
        c.wait_recv()
    l4[y] = sum([l3[k] for k in range(1, 4)], l3[0])
    start(*loss_col)
    ring_back(6)
    send_home(2)
    for c in loss_col:
        c.wait_recv()
    total = sum([l4[k] for k in range(1, 4)], l4[0])
    pairs = N * 256
    loss_out[0] = jnp.sum(total[0:8]) / pairs
    bias_out[0] = jnp.sum(total[8:16]) / pairs

    for k in (5, 6):
        back_left[k].wait_recv()
        back_right[k].wait_recv()
    for half in (0, 1):
        rows = slice(half * H, half * H + H)
        side_l = zl_recv[6 if half == 0 else 5].astype(F32)
        side_r = zr_recv[5 if half == 0 else 6].astype(F32)
        gy = temp * (g_t[3, rows] + side_l + side_r + own_cb[rows] * x_low[rows])
        yu = y_unit[rows]
        text_grad[rows] = (gy - yu * jnp.sum(yu * gy, axis=-1, keepdims=True)) * y_inverse[rows]

    gx = gather_across(0) + own_cb * y_low
    for r in (1, 3, 2):
        back_direct[r].wait_recv()
        gx = gx + dr_recv[r - 1].astype(F32)
    gx = temp * gx
    image_grad[...] = (gx - x_unit * jnp.sum(x_unit * gx, axis=-1, keepdims=True)) * x_inverse

    for c in started:
        c.wait_send()


def per_device(images, texts, log_temp, bias):
    N, W = images.shape
    H = N // 2
    vmem = pl.BlockSpec(memory_space=pltpu.VMEM)
    smem = pl.BlockSpec(memory_space=pltpu.SMEM)
    scratch = [
        pltpu.VMEM((8, 2 * N, W), BF16),
        pltpu.VMEM((4, 2 * N, W), BF16),
        pltpu.VMEM((8, 2 * N, W), F32),
        pltpu.VMEM((4, 2 * N, W), F32),
        pltpu.VMEM((2 * N, 2 * N), BF16),
        pltpu.VMEM((2 * N, 2 * N), BF16),
        pltpu.VMEM((2, 2 * N, 2 * N), F32),
        pltpu.VMEM((2, 8, 2 * N), F32),
        pltpu.VMEM((8, N, W), BF16),
        pltpu.VMEM((8, N, W), BF16),
        pltpu.VMEM((4, N, W), BF16),
        pltpu.VMEM((4, N, W), BF16),
        pltpu.VMEM((3, N, W), BF16),
        pltpu.VMEM((3, N, W), BF16),
        pltpu.VMEM((7, H, W), BF16),
        pltpu.VMEM((7, H, W), BF16),
        pltpu.VMEM((7, H, W), BF16),
        pltpu.VMEM((7, H, W), BF16),
        pltpu.VMEM((2, 16, 128), F32),
        pltpu.VMEM((8, 16, 128), F32),
        pltpu.VMEM((4, 16, 128), F32),
        pltpu.VMEM((4, 16, 128), F32),
        pltpu.SemaphoreType.DMA((80,)),
        pltpu.SemaphoreType.DMA((80,)),
    ]
    return pl.pallas_call(
        kernel,
        out_shape=(
            jax.ShapeDtypeStruct((N, W), F32),
            jax.ShapeDtypeStruct((N, W), F32),
            jax.ShapeDtypeStruct((1,), F32),
            jax.ShapeDtypeStruct((1,), F32),
        ),
        in_specs=[vmem, vmem, smem, smem],
        out_specs=(vmem, vmem, smem, smem),
        scratch_shapes=scratch,
        compiler_params=pltpu.CompilerParams(
            collective_id=0, has_side_effects=True, vmem_limit_bytes=58 * 1024 * 1024
        ),
    )(images, texts, log_temp, bias)


def solution(mesh):
    placed = (P(("grp", "mem"), None), P(("grp", "mem"), None), P(), P())
    return jax.shard_map(
        per_device,
        mesh=mesh,
        in_specs=placed,
        out_specs=(P(("grp", "mem"), None), P(("grp", "mem"), None), P(), P()),
        check_vma=False,
    )
```

```python
import functools
import math

import jax
import jax.numpy as jnp
from jax import lax
from jax.experimental import pallas as pl
from jax.experimental.pallas import tpu as pltpu
from jax.sharding import PartitionSpec as P

MESH = pl.DeviceIdType.MESH
F32 = jnp.float32
BF16 = jnp.bfloat16
LOG2E = math.log2(math.e)
LN2 = math.log(2.0)
SIDE = 64
SIDE_A = 32
MESSAGES_OUT = 40
MESSAGES = 93
SEND_SEMAPHORES = MESSAGES - MESSAGES_OUT


P_SLOT = {0: 0, 1: 2, 3: 3, 2: 6}
S_SLOT = {0: 1, 1: 4, 3: 5, 2: 7}
T_PLACE = {"R1": (0, 0), "L1": (0, 1), "R2": (1, 0), "L2": (1, 1), "R3": (2, 0), "L3": (2, 1), "R0": (3, 0), "L0": (3, 0), "R4": (3, 1), "L4": (3, 1)}


UNITS = (
    (0, 0), (1, 0), (0, 1), (1, 1), (2, 0), (2, 1), (0, 2), (1, 2),
    (2, 2), (3, 0), (3, 1), (3, 2), (3, 3), (2, 3), (1, 3), (0, 3),
)


def unit_of(n):
    p, q = UNITS[0]
    for k in range(1, len(UNITS)):
        p = jnp.where(n == k, UNITS[k][0], p)
        q = jnp.where(n == k, UNITS[k][1], q)
    return p, q


def log1p_sum(q):
    series = q * (1.0 - q * (0.5 - q * (1.0 / 3.0 - q * 0.25)))
    return jnp.where(q < 0.0078125, series, jnp.log(1.0 + q))


def kernel(
    images, texts, log_temp, bias,
    image_grad, text_grad, loss_out, bias_out,
    ibuf, tbuf, tt, g_i, g_t, cbuf, ctbuf, shift, sums, own_weight,
    tw_send, tw_recv, pt_send, pt_recv, dr_send, dr_recv, xa_send, xa_recv, f_send, f_recv,
    sx_send, sx_recv, xs_send, xs_recv, sf_send, sf_recv,
    zl_send, zl_recv, zr_send, zr_recv,
    l1, l2, l3, l4, ssem, rsem,
):
    N, W = images.shape
    H = N // 2
    A = N - SIDE
    C = A + SIDE_A
    g = lax.axis_index("grp")
    m = lax.axis_index("mem")
    y = lax.rem(g, 4)
    xh = lax.div(g, 4)
    xl = lax.div(m, 16)
    z = lax.rem(lax.div(m, 2), 8)
    core = lax.rem(m, 2)
    x = xh * 2 + xl

    def dev(x_hi, yy, x_lo, zz, cc):
        return (x_hi * 4 + lax.rem(yy, 4), x_lo * 16 + lax.rem(zz, 8) * 2 + cc)

    twin = dev(xh, y, xl, z, 1 - core)
    ring = [dev(xh, y, xl, z + k, core) for k in range(8)]
    ahead, back = ring[1], ring[7]
    partner = dev(xh, y, 1 - xl, z, core)
    adjacent = dev(1 - xh, y, 1 - xl, z, core)
    far = dev(1 - xh, y, xl, z, core)
    north, across_y, south = (dev(xh, y + k, xl, z, core) for k in (1, 2, 3))
    up = dev(jnp.where(y == 3, 1 - xh, xh), y + 1, jnp.where(y == 3, 1 - xl, xl), z, core)
    down = dev(jnp.where(y == 0, 1 - xh, xh), y + 3, jnp.where(y == 0, 1 - xl, xl), z, core)

    count = [0]
    started = []

    def message(src, dst, device):
        i = count[0]
        count[0] += 1
        return pltpu.make_async_remote_copy(
            src_ref=src, dst_ref=dst, send_sem=ssem.at[i if i < MESSAGES_OUT else i - MESSAGES_OUT], recv_sem=rsem.at[i],
            device_id=device, device_id_type=MESH,
        )

    def start(*copies):
        for c in copies:
            c.start()
            started.append(c)

    def start_if(where, *copies):
        for c in copies:
            pl.when(where)(c.start)

    def place(name, half):
        q, at = T_PLACE[name]
        return tbuf.at[q, pl.ds(at * N + half * H, H)]

    right, left = [], []
    for k in range(7):
        a, b_ = k // 2, k // 2 + 1
        right.append(message(place(f"R{a}", k % 2), place(f"R{b_}", k % 2), ahead))
        left.append(message(place(f"L{a}", 1 - k % 2), place(f"L{b_}", 1 - k % 2), back))

    def rows_of(b, lo, hi):
        return ibuf.at[b, pl.ds(lo, hi - lo)]

    def move(src, dst, lo, hi, device):
        return message(rows_of(src, lo, hi), rows_of(dst, lo, hi), device)

    halves = ((0, H), (H, N))
    go_north, go_south = jnp.where(y < 3, 8, 0), jnp.where(y == 0, 8, 0)
    swap = [move(0, 8, lo, hi, adjacent) for lo, hi in halves]
    direct = {1: [move(go_north, P_SLOT[1], lo, hi, north) for lo, hi in halves], 3: [move(go_south, P_SLOT[3], lo, hi, south) for lo, hi in halves]}

    direct2 = [move(P_SLOT[1], P_SLOT[2], 0, H, up), move(P_SLOT[3], P_SLOT[2], H, N, down)]
    across = {0: [move(0, S_SLOT[0], lo, hi, partner) for lo, hi in ((A, N), (0, A))]}
    for r in (1, 3, 2):
        across[r] = [move(P_SLOT[r], S_SLOT[r], 0, A, partner)]
    side_swap = move(S_SLOT[0], 9, A, N, adjacent)
    side = {
        1: move(jnp.where(y < 3, 9, S_SLOT[0]), S_SLOT[1], A, N, north),
        3: move(jnp.where(y == 0, 9, S_SLOT[0]), S_SLOT[3], A, N, south),
    }
    side2 = [move(S_SLOT[1], S_SLOT[2], A, C, up), move(S_SLOT[3], S_SLOT[2], C, N, down)]
    twins = [message(rows_of(b, 0, N), rows_of(b, N, 2 * N), twin) for b in range(8)]

    assert count[0] == MESSAGES_OUT
    back_twin = [message(tw_send.at[b], tw_recv.at[b], twin) for b in range(8)]
    back_across = {
        r: message(pt_send.at[r, pl.ds(0, N if r == 0 else A)], pt_recv.at[r, pl.ds(0, N if r == 0 else A)], partner)
        for r in range(4)
    }
    back_direct = {
        r: [message(dr_send.at[i, pl.ds(lo, H)], dr_recv.at[i, pl.ds(lo, H)], d) for lo in (0, H)]
        for i, r, d in ((0, 1, south), (1, 3, north))
    }
    back_swap = [message(xa_send.at[pl.ds(lo, H)], xa_recv.at[pl.ds(lo, H)], adjacent) for lo in (0, H)]
    back_side = {r: message(sx_send.at[i], sx_recv.at[i], d) for i, r, d in ((0, 1, south), (1, 3, north))}
    back_side_swap = message(xs_send, xs_recv, adjacent)

    back_direct2 = [message(f_send.at[i], f_recv.at[i], d) for i, d in ((0, down), (1, up))]
    back_side2 = [message(sf_send.at[i], sf_recv.at[i], d) for i, d in ((0, down), (1, up))]
    back_left = [message(zl_send.at[k], zl_recv.at[k], back) for k in range(7)]
    back_right = [message(zr_send.at[k], zr_recv.at[k], ahead) for k in range(7)]
    loss_twin = message(l1.at[0], l1.at[1], twin)
    loss_ring = [message(l2.at[z], l2.at[z], ring[k]) for k in range(1, 8)]
    loss_row = [message(l3.at[x], l3.at[x], d) for d in (partner, adjacent, far)]
    loss_col = [message(l4.at[y], l4.at[y], d) for d in (north, across_y, south)]

    far_north, far_south = dev(1 - xh, y + 1, 1 - xl, z, core), dev(1 - xh, y + 3, 1 - xl, z, core)

    peers = [twin, *ring[1:], partner, adjacent, far, north, across_y, south, far_north, far_south]
    barrier = pltpu.get_barrier_semaphore()
    for p in peers:
        pl.semaphore_signal(barrier, inc=1, device_id=p, device_id_type=MESH)

    def unit_rows(ref):
        full = ref[...].astype(F32)
        inverse = lax.rsqrt(jnp.sum(full * full, axis=-1, keepdims=True) + 1e-06)
        return full * inverse, inverse

    tbuf[3, 0:N] = unit_rows(texts)[0].astype(BF16)
    ibuf[0, 0:N] = unit_rows(images)[0].astype(BF16)
    pl.semaphore_wait(barrier, len(peers))
    start(right[0], left[0], swap[0], across[0][0])
    start_if(y > 0, direct[3][0])
    start_if(y == 3, direct[1][0])
    start(right[1], left[1], swap[1], across[0][1])
    start_if(y > 0, direct[3][1])
    start_if(y == 3, direct[1][1])
    start(twins[0])
    started.extend(direct[1] + direct[3] + list(side.values()))

    temp = jnp.max(jnp.exp(jnp.full((8, 128), log_temp[0], F32)))
    offset = bias[0]
    scale = temp * LOG2E
    offset2 = offset * LOG2E
    row = lax.broadcasted_iota(jnp.int32, (4 * N, 2 * N), 0)
    col = lax.broadcasted_iota(jnp.int32, (4 * N, 2 * N), 1)
    shift[0] = jnp.full((4 * N, 2 * N), offset2, F32)
    shift[1] = jnp.where((row == col) & (row < N), -1e30, offset2)

    def clear(i, carry):
        zeros = jnp.zeros((32, W), F32)
        g_i[lax.div(i, 8), pl.ds(pl.multiple_of(lax.rem(i, 8) * 32, 32), 32)] = zeros

        @pl.when(i < 32)
        def _():
            g_t[lax.div(i, 8), pl.ds(pl.multiple_of(lax.rem(i, 8) * 32, 32), 32)] = zeros

        return carry

    lax.fori_loop(0, 64, clear, 0)

    positive = temp * jnp.sum(ibuf[0, 0:N].astype(F32) * tbuf[3, 0:N].astype(F32), axis=-1, keepdims=True) + offset
    e_own = jnp.exp(-jnp.abs(positive))
    own_c = -jnp.where(positive >= 0.0, e_own, 1.0) / (1.0 + e_own)
    own_loss = jnp.maximum(-positive, 0.0) + log1p_sum(e_own)
    own_weight[...] = jnp.broadcast_to(own_c.astype(BF16).astype(F32), (N, 128))
    first = lax.broadcasted_iota(jnp.int32, (8, 2 * N), 0) + lax.broadcasted_iota(jnp.int32, (8, 2 * N), 1) == 0
    sums[0] = jnp.where(first, jnp.sum(own_loss), 0.0)
    sums[1] = jnp.where(first, jnp.sum(own_c), 0.0)
    tt[3, :, 0:N] = tbuf[3, 0:N].T

    def hop(k):
        right[k].wait_recv()
        left[k].wait_recv()
        if k + 2 < 7:
            start(right[k + 2], left[k + 2])

    def logits(p, q):
        return jnp.dot(ibuf[pl.ds(2 * p, 2)].reshape(4 * N, W), tt[q], preferred_element_type=F32)

    def weights(dots, masked):
        u = dots * scale + shift[masked]
        e = jnp.exp2(-jnp.abs(u))
        d = 1.0 + e
        inv = pl.reciprocal(d, approx=True)
        inv = inv * (2.0 - d * inv)
        c = jnp.where(u >= 0.0, 1.0, e) * inv
        cb = c.astype(BF16)
        cbuf[...] = cb
        ctbuf[...] = cb.T
        parts = [e[8 * i : 8 * i + 8] for i in range(4 * N // 8)]
        while len(parts) > 1:
            parts = [a + (h + a * h) for a, h in zip(parts[::2], parts[1::2])]
        tail = log1p_sum(parts[0])
        linear = jnp.sum(jnp.maximum(u, 0.0).reshape(4 * N // 8, 8, 2 * N), axis=0)
        csum = jnp.sum(c.reshape(4 * N // 8, 8, 2 * N), axis=0)
        sums[0] += tail + linear * LN2
        sums[1] += csum

    def grads(p, q):
        c, ct = cbuf[...], ctbuf[...]
        for lo, hi in ((0, W),):
            g_i[pl.ds(2 * p, 2), :, lo:hi] += jnp.dot(c, tbuf[q, :, lo:hi], preferred_element_type=F32).reshape(2, 2 * N, hi - lo)
            g_t[q, :, lo:hi] += jnp.dot(
                ct, ibuf[pl.ds(2 * p, 2), :, lo:hi].reshape(4 * N, hi - lo), preferred_element_type=F32
            )

    def text_part(name, half):
        q, at = T_PLACE[name]
        return g_t[q, at * N + half * H : at * N + half * H + H]

    def ring_back(k):
        name = 4 - (k + 1) // 2
        for sign, send, recv, out in (("R", zl_send, zl_recv, back_left), ("L", zr_send, zr_recv, back_right)):
            half = (k % 2) if sign == "R" else 1 - (k % 2)
            share = text_part(f"{sign}{name}", half)
            if k >= 2:
                out[k - 2].wait_recv()
                share = share + recv[k - 2].astype(F32)
            send[k] = share.astype(BF16)
            start(out[k])

    def shared(b, lo, hi):
        return g_i[b, lo:hi] + tw_recv[b, lo:hi].astype(F32)

    def leave_second():
        back_twin[7].wait_recv()
        sf_send[0, 0:SIDE_A] = shared(7, A, C).astype(BF16)
        sf_send[1, 0 : SIDE - SIDE_A] = shared(7, C, N).astype(BF16)
        start(*back_side2)
        pt_send[2, 0:A] = shared(7, 0, A).astype(BF16)
        start(back_across[2])

    def to_twin(b):
        tw_send[b] = g_i[b, N : 2 * N].astype(BF16)
        start(back_twin[b])

    def swapped(i):
        swap[i].wait_recv()
        start_if(y < 3, direct[1][i])
        start_if(y == 0, direct[3][i])

    def arrived(i):
        for r in (1, 3):
            direct[r][i].wait_recv()
        if i == 0:
            start(across[1][0], across[3][0], direct2[0])
        else:
            start(direct2[1], twins[P_SLOT[1]], twins[P_SLOT[3]])

    swapped(0)
    across[0][0].wait_recv()
    start(side_swap)
    start_if(y > 0, side[3])
    start_if(y == 3, side[1])
    hop(0)
    swapped(1)
    hop(1)
    side_swap.wait_recv()
    start_if(y < 3, side[1])
    start_if(y == 0, side[3])
    across[0][1].wait_recv()
    start(twins[S_SLOT[0]])
    arrived(0)
    tt[0] = tbuf[0].T
    twins[0].wait_recv()
    twins[1].wait_recv()

    def step(n, carry):
        @pl.when(n == 1)
        def _():
            arrived(1)
            hop(2)
            side[1].wait_recv()
            side[3].wait_recv()
            start(*side2)
            twins[2].wait_recv()
            twins[3].wait_recv()

        @pl.when(n == 2)
        def _():
            direct2[0].wait_recv()
            start(across[2][0])
            hop(3)
            across[1][0].wait_recv()
            across[3][0].wait_recv()
            start(twins[S_SLOT[1]], twins[S_SLOT[3]])
            tt[1] = tbuf[1].T

        @pl.when(n == 4)
        def _():
            direct2[1].wait_recv()
            start(twins[P_SLOT[2]])
            hop(4)
            twins[4].wait_recv()
            twins[5].wait_recv()

        @pl.when(n == 6)
        def _():
            side2[0].wait_recv()
            side2[1].wait_recv()
            across[2][0].wait_recv()
            start(twins[S_SLOT[2]])
            hop(5)
            tt[2] = tbuf[2].T

        @pl.when(n == 9)
        def _():
            twins[6].wait_recv()
            twins[7].wait_recv()

        @pl.when(n == 12)
        def _():
            hop(6)
            tt[3, :, N : 2 * N] = tbuf[3, N : 2 * N].T

        @pl.when(n == 13)
        def _():
            for c in started:
                c.wait_send()
            started.clear()
            ring_back(1)

        @pl.when(n == 14)
        def _():
            to_twin(7)
            to_twin(6)

        @pl.when(n == 15)
        def _():
            to_twin(4)
            to_twin(5)

        p, q = unit_of(n)
        before_p, before_q = unit_of(n - 1)
        dots = logits(p, q)
        grads(before_p, before_q)
        weights(dots, jnp.where(n == 15, 1, 0))
        return carry

    weights(logits(0, 0), 0)
    lax.fori_loop(1, 16, step, 0)
    grads(0, 3)

    def home(r, lo, hi):
        crossed = N if r == 0 else A
        if hi <= crossed:
            return shared(P_SLOT[r], lo, hi) + pt_recv[r, lo:hi].astype(F32)
        if lo >= crossed:
            return shared(P_SLOT[r], lo, hi)
        return jnp.concatenate([home(r, lo, crossed), home(r, crossed, hi)], axis=0)

    def keep(where, values):
        return jnp.where(where, values.astype(F32), 0.0)

    ring_back(0)
    for b in (2, 3, 1, 0):
        to_twin(b)
    l1[0, 0:8] = sums[0, :, 0:128] + sums[0, :, 128:256]
    l1[0, 8:16] = sums[1, :, 0:128] + sums[1, :, 128:256]
    start(loss_twin)

    leave_second()
    for r in (1, 3):
        back_twin[S_SLOT[r]].wait_recv()
        pt_send[r, 0:A] = shared(S_SLOT[r], 0, A).astype(BF16)
        start(back_across[r])
    ring_back(2)

    for i, r in ((0, 1), (1, 3)):
        b = S_SLOT[r]
        plain, joined = (slice(C, N), slice(A, C)) if i == 0 else (slice(A, C), slice(C, N))
        sx_send[i, plain.start - A : plain.stop - A] = shared(b, plain.start, plain.stop).astype(BF16)
        back_side2[i].wait_recv()
        sx_send[i, joined.start - A : joined.stop - A] = (shared(b, joined.start, joined.stop) + sf_recv[i].astype(F32)).astype(BF16)
        start(back_side[r])
    back_twin[P_SLOT[2]].wait_recv()
    back_across[2].wait_recv()
    f_send[0] = home(2, 0, H).astype(BF16)
    f_send[1] = home(2, H, N).astype(BF16)
    start(*back_direct2)
    loss_twin.wait_recv()
    l2[z] = l1[0] + l1[1]
    start(*loss_ring)
    ring_back(3)
    for r in (1, 3):
        back_side[r].wait_recv()
    xs_send[...] = (keep(y < 3, sx_recv[0]) + keep(y == 0, sx_recv[1])).astype(BF16)
    start(back_side_swap)

    def send_home(r):
        i = r // 2
        back_twin[P_SLOT[r]].wait_recv()
        back_across[r].wait_recv()
        for k in (1 - i, i):
            lo, hi = halves[k]
            share = home(r, lo, hi)
            if k == i:
                back_direct2[i].wait_recv()
                share = share + f_recv[i].astype(F32)
            dr_send[i, lo:hi] = share.astype(BF16)
            start(back_direct[r][k])

    send_home(1)
    ring_back(4)
    send_home(3)
    for c in loss_ring:
        c.wait_recv()
    l3[x] = sum([l2[k] for k in range(1, 8)], l2[0])
    start(*loss_row)
    back_twin[1].wait_recv()
    back_side_swap.wait_recv()
    pt_send[0, 0:A] = shared(1, 0, A).astype(BF16)
    side_sum = keep(y == 3, sx_recv[0]) + keep(y > 0, sx_recv[1]) + xs_recv[...].astype(F32)
    pt_send[0, A:N] = (shared(1, A, N) + side_sum).astype(BF16)
    start(back_across[0])
    ring_back(5)

    def swap_home(k):
        lo, hi = halves[k]
        back_direct[1][k].wait_recv()

        @pl.when(y == 0)
        def _():
            back_direct[3][k].wait_recv()
            xa_send[lo:hi] = (dr_recv[0, lo:hi].astype(F32) + dr_recv[1, lo:hi].astype(F32)).astype(BF16)

        @pl.when(y > 0)
        def _():
            xa_send[lo:hi] = keep(y < 3, dr_recv[0, lo:hi]).astype(BF16)

        start(back_swap[k])

    swap_home(0)
    ring_back(6)
    swap_home(1)
    for c in loss_row:
        c.wait_recv()
    l4[y] = sum([l3[k] for k in range(1, 4)], l3[0])
    start(*loss_col)
    x_unit, x_inverse = unit_rows(images)
    y_unit, y_inverse = unit_rows(texts)
    own_cb = own_weight[:, 0:1]
    for half in (1, 0):
        rows = slice(half * H, half * H + H)
        back_left[6 - half].wait_recv()
        back_right[5 + half].wait_recv()
        came = zl_recv[6 - half].astype(F32) + zr_recv[5 + half].astype(F32)
        gy = temp * (g_t[3, rows] + came + own_cb[rows] * ibuf[0, rows].astype(F32))
        yu = y_unit[rows]
        text_grad[rows] = (gy - yu * jnp.sum(yu * gy, axis=-1, keepdims=True)) * y_inverse[rows]

    back_twin[0].wait_recv()
    back_across[0].wait_recv()
    for k, (lo, hi) in enumerate(halves):
        back_swap[k].wait_recv()
        pl.when(y > 0)(back_direct[3][k].wait_recv)
        came = keep(y == 3, dr_recv[0, lo:hi]) + keep(y > 0, dr_recv[1, lo:hi]) + xa_recv[lo:hi].astype(F32)
        gx = temp * (home(0, lo, hi) + own_cb[lo:hi] * tbuf[3, lo:hi].astype(F32) + came)
        xu = x_unit[lo:hi]
        image_grad[lo:hi] = (gx - xu * jnp.sum(xu * gx, axis=-1, keepdims=True)) * x_inverse[lo:hi]

    for c in loss_col:
        c.wait_recv()
    total = sum([l4[k] for k in range(1, 4)], l4[0])
    pairs = N * 256
    loss_out[...] = jnp.full((1,), jnp.sum(total[0:8]) / pairs, F32)
    bias_out[...] = jnp.full((1,), jnp.sum(total[8:16]) / pairs, F32)

    for c in started:
        c.wait_send()


def per_device(images, texts, log_temp, bias):
    N, W = images.shape
    H = N // 2
    vmem = pl.BlockSpec(memory_space=pltpu.VMEM)
    smem = pl.BlockSpec(memory_space=pltpu.SMEM)
    scratch = [
        pltpu.VMEM((10, 2 * N, W), BF16),
        pltpu.VMEM((4, 2 * N, W), BF16),
        pltpu.VMEM((4, W, 2 * N), BF16),
        pltpu.VMEM((8, 2 * N, W), F32),
        pltpu.VMEM((4, 2 * N, W), F32),
        pltpu.VMEM((4 * N, 2 * N), BF16),
        pltpu.VMEM((2 * N, 4 * N), BF16),
        pltpu.VMEM((2, 4 * N, 2 * N), F32),
        pltpu.VMEM((2, 8, 2 * N), F32),
        pltpu.VMEM((N, 128), F32),
        *[pltpu.VMEM((8, N, W), BF16)] * 2,
        *[pltpu.VMEM((4, N, W), BF16)] * 2,
        *[pltpu.VMEM((2, N, W), BF16)] * 2,
        *[pltpu.VMEM((N, W), BF16)] * 2,
        *[pltpu.VMEM((2, H, W), BF16)] * 2,
        *[pltpu.VMEM((2, SIDE, W), BF16)] * 2,
        *[pltpu.VMEM((SIDE, W), BF16)] * 2,
        *[pltpu.VMEM((2, SIDE_A, W), BF16)] * 2,
        *[pltpu.VMEM((7, H, W), BF16)] * 4,
        pltpu.VMEM((2, 16, 128), F32),
        pltpu.VMEM((8, 16, 128), F32),
        pltpu.VMEM((4, 16, 128), F32),
        pltpu.VMEM((4, 16, 128), F32),
        pltpu.SemaphoreType.DMA((SEND_SEMAPHORES,)),
        pltpu.SemaphoreType.DMA((MESSAGES,)),
    ]
    return pl.pallas_call(
        kernel,
        out_shape=(
            jax.ShapeDtypeStruct((N, W), F32),
            jax.ShapeDtypeStruct((N, W), F32),
            jax.ShapeDtypeStruct((1,), F32),
            jax.ShapeDtypeStruct((1,), F32),
        ),
        in_specs=[vmem, vmem, smem, smem],
        out_specs=(vmem, vmem, vmem, vmem),
        scratch_shapes=scratch,
        compiler_params=pltpu.CompilerParams(
            collective_id=0, has_side_effects=True, vmem_limit_bytes=46 * 1024 * 1024
        ),
    )(images, texts, log_temp, bias)


def solution(mesh):
    placed = (P(("grp", "mem"), None), P(("grp", "mem"), None), P(), P())
    return jax.shard_map(
        per_device,
        mesh=mesh,
        in_specs=placed,
        out_specs=(P(("grp", "mem"), None), P(("grp", "mem"), None), P(), P()),
        check_vma=False,
    )
```

```python
import functools
import math

import jax
import jax.numpy as jnp
from jax import lax
from jax.experimental import pallas as pl
from jax.experimental.pallas import tpu as pltpu
from jax.sharding import PartitionSpec as P

MESH = pl.DeviceIdType.MESH
F32 = jnp.float32
BF16 = jnp.bfloat16
LOG2E = math.log2(math.e)
LN2 = math.log(2.0)
SIDE = 64
SIDE_A = 32
MESSAGES_OUT = 40
MESSAGES = 94
SEND_SEMAPHORES = MESSAGES - MESSAGES_OUT


P_SLOT = {0: 0, 1: 2, 3: 3, 2: 6}
S_SLOT = {0: 1, 1: 4, 3: 5, 2: 7}
T_PLACE = {"R1": (0, 0), "L1": (0, 1), "R2": (1, 0), "L2": (1, 1), "R3": (2, 0), "L3": (2, 1), "R0": (3, 0), "L0": (3, 0), "R4": (3, 1), "L4": (3, 1)}


UNITS = (
    (0, 0), (1, 0), (0, 1), (1, 1), (2, 0), (2, 1), (0, 2), (1, 2),
    (2, 2), (3, 0), (3, 1), (3, 2), (3, 3), (2, 3), (1, 3), (0, 3),
)


def unit_of(n):
    p, q = UNITS[0]
    for k in range(1, len(UNITS)):
        p = jnp.where(n == k, UNITS[k][0], p)
        q = jnp.where(n == k, UNITS[k][1], q)
    return p, q


def log1p_sum(q):
    series = q * (1.0 - q * (0.5 - q * (1.0 / 3.0 - q * 0.25)))
    return jnp.where(q < 0.0078125, series, jnp.log(1.0 + q))


def kernel(
    images, texts, log_temp, bias,
    image_grad, text_grad, loss_out, bias_out,
    ibuf, tbuf, tt, g_i, g_t, cbuf, ctbuf, shift, sums, own_weight,
    tw_send, tw_recv, pt_send, pt_recv, dr_send, dr_recv, xa_send, xa_recv, f_send, f_recv,
    sx_send, sx_recv, xs_send, xs_recv, sf_send, sf_recv,
    zl_send, zl_recv, zr_send, zr_recv,
    l1, l2, l3, l4, ssem, rsem,
):
    N, W = images.shape
    H = N // 2
    A = N - SIDE
    C = A + SIDE_A
    g = lax.axis_index("grp")
    m = lax.axis_index("mem")
    y = lax.rem(g, 4)
    xh = lax.div(g, 4)
    xl = lax.div(m, 16)
    z = lax.rem(lax.div(m, 2), 8)
    core = lax.rem(m, 2)
    x = xh * 2 + xl

    def dev(x_hi, yy, x_lo, zz, cc):
        return (x_hi * 4 + lax.rem(yy, 4), x_lo * 16 + lax.rem(zz, 8) * 2 + cc)

    twin = dev(xh, y, xl, z, 1 - core)
    ring = [dev(xh, y, xl, z + k, core) for k in range(8)]
    ahead, back = ring[1], ring[7]
    partner = dev(xh, y, 1 - xl, z, core)
    adjacent = dev(1 - xh, y, 1 - xl, z, core)
    far = dev(1 - xh, y, xl, z, core)
    north, across_y, south = (dev(xh, y + k, xl, z, core) for k in (1, 2, 3))
    up = dev(jnp.where(y == 3, 1 - xh, xh), y + 1, jnp.where(y == 3, 1 - xl, xl), z, core)
    down = dev(jnp.where(y == 0, 1 - xh, xh), y + 3, jnp.where(y == 0, 1 - xl, xl), z, core)

    count = [0]
    started = []

    def message(src, dst, device):
        i = count[0]
        count[0] += 1
        return pltpu.make_async_remote_copy(
            src_ref=src, dst_ref=dst, send_sem=ssem.at[i if i < MESSAGES_OUT else i - MESSAGES_OUT], recv_sem=rsem.at[i],
            device_id=device, device_id_type=MESH,
        )

    def start(*copies):
        for c in copies:
            c.start()
            started.append(c)

    def start_if(where, *copies):
        for c in copies:
            pl.when(where)(c.start)

    def place(name, half):
        q, at = T_PLACE[name]
        return tbuf.at[q, pl.ds(at * N + half * H, H)]

    right, left = [], []
    for k in range(7):
        a, b_ = k // 2, k // 2 + 1
        right.append(message(place(f"R{a}", k % 2), place(f"R{b_}", k % 2), ahead))
        left.append(message(place(f"L{a}", 1 - k % 2), place(f"L{b_}", 1 - k % 2), back))

    def rows_of(b, lo, hi):
        return ibuf.at[b, pl.ds(lo, hi - lo)]

    def move(src, dst, lo, hi, device):
        return message(rows_of(src, lo, hi), rows_of(dst, lo, hi), device)

    halves = ((0, H), (H, N))
    go_north, go_south = jnp.where(y < 3, 8, 0), jnp.where(y == 0, 8, 0)
    swap = [move(0, 8, lo, hi, adjacent) for lo, hi in halves]
    direct = {1: [move(go_north, P_SLOT[1], lo, hi, north) for lo, hi in halves], 3: [move(go_south, P_SLOT[3], lo, hi, south) for lo, hi in halves]}

    direct2 = [move(P_SLOT[1], P_SLOT[2], 0, H, up), move(P_SLOT[3], P_SLOT[2], H, N, down)]
    across = {0: [move(0, S_SLOT[0], lo, hi, partner) for lo, hi in ((A, N), (0, A))]}
    for r in (1, 3, 2):
        across[r] = [move(P_SLOT[r], S_SLOT[r], 0, A, partner)]
    side_swap = move(S_SLOT[0], 9, A, N, adjacent)
    side = {
        1: move(jnp.where(y < 3, 9, S_SLOT[0]), S_SLOT[1], A, N, north),
        3: move(jnp.where(y == 0, 9, S_SLOT[0]), S_SLOT[3], A, N, south),
    }
    side2 = [move(S_SLOT[1], S_SLOT[2], A, C, up), move(S_SLOT[3], S_SLOT[2], C, N, down)]
    twins = [message(rows_of(b, 0, N), rows_of(b, N, 2 * N), twin) for b in range(8)]

    assert count[0] == MESSAGES_OUT
    back_twin = [message(tw_send.at[b], tw_recv.at[b], twin) for b in range(8)]
    back_across = {r: message(pt_send.at[r, pl.ds(0, A)], pt_recv.at[r, pl.ds(0, A)], partner) for r in range(4)}
    back_across_rest = message(pt_send.at[0, pl.ds(A, SIDE)], pt_recv.at[0, pl.ds(A, SIDE)], partner)
    back_direct = {
        r: [message(dr_send.at[i, pl.ds(lo, H)], dr_recv.at[i, pl.ds(lo, H)], d) for lo in (0, H)]
        for i, r, d in ((0, 1, south), (1, 3, north))
    }
    back_swap = [message(xa_send.at[pl.ds(lo, H)], xa_recv.at[pl.ds(lo, H)], adjacent) for lo in (0, H)]
    back_side = {r: message(sx_send.at[i], sx_recv.at[i], d) for i, r, d in ((0, 1, south), (1, 3, north))}
    back_side_swap = message(xs_send, xs_recv, adjacent)

    back_direct2 = [message(f_send.at[i], f_recv.at[i], d) for i, d in ((0, down), (1, up))]
    back_side2 = [message(sf_send.at[i], sf_recv.at[i], d) for i, d in ((0, down), (1, up))]
    back_left = [message(zl_send.at[k], zl_recv.at[k], back) for k in range(7)]
    back_right = [message(zr_send.at[k], zr_recv.at[k], ahead) for k in range(7)]
    loss_twin = message(l1.at[0], l1.at[1], twin)
    loss_ring = [message(l2.at[z], l2.at[z], ring[k]) for k in range(1, 8)]
    loss_row = [message(l3.at[x], l3.at[x], d) for d in (partner, adjacent, far)]
    loss_col = [message(l4.at[y], l4.at[y], d) for d in (north, across_y, south)]

    far_north, far_south = dev(1 - xh, y + 1, 1 - xl, z, core), dev(1 - xh, y + 3, 1 - xl, z, core)

    peers = [twin, *ring[1:], partner, adjacent, far, north, across_y, south, far_north, far_south]
    barrier = pltpu.get_barrier_semaphore()
    for p in peers:
        pl.semaphore_signal(barrier, inc=1, device_id=p, device_id_type=MESH)

    def unit_rows(ref):
        full = ref[...].astype(F32)
        inverse = lax.rsqrt(jnp.sum(full * full, axis=-1, keepdims=True) + 1e-06)
        return full * inverse, inverse

    tbuf[3, 0:N] = unit_rows(texts)[0].astype(BF16)
    ibuf[0, 0:N] = unit_rows(images)[0].astype(BF16)
    pl.semaphore_wait(barrier, len(peers))
    start(right[0], left[0], swap[0], across[0][0])
    start_if(y > 0, direct[3][0])
    start_if(y == 3, direct[1][0])
    start(right[1], left[1], swap[1], across[0][1])
    start_if(y > 0, direct[3][1])
    start_if(y == 3, direct[1][1])
    start(twins[0])
    started.extend(direct[1] + direct[3] + list(side.values()))

    temp = jnp.max(jnp.exp(jnp.full((8, 128), log_temp[0], F32)))
    offset = bias[0]
    scale = temp * LOG2E
    offset2 = offset * LOG2E
    row = lax.broadcasted_iota(jnp.int32, (4 * N, 2 * N), 0)
    col = lax.broadcasted_iota(jnp.int32, (4 * N, 2 * N), 1)
    shift[0] = jnp.full((4 * N, 2 * N), offset2, F32)
    shift[1] = jnp.where((row == col) & (row < N), -1e30, offset2)

    def clear(i, carry):
        zeros = jnp.zeros((32, W), F32)
        g_i[lax.div(i, 8), pl.ds(pl.multiple_of(lax.rem(i, 8) * 32, 32), 32)] = zeros

        @pl.when(i < 32)
        def _():
            g_t[lax.div(i, 8), pl.ds(pl.multiple_of(lax.rem(i, 8) * 32, 32), 32)] = zeros

        return carry

    lax.fori_loop(0, 64, clear, 0)

    positive = temp * jnp.sum(ibuf[0, 0:N].astype(F32) * tbuf[3, 0:N].astype(F32), axis=-1, keepdims=True) + offset
    e_own = jnp.exp(-jnp.abs(positive))
    own_c = -jnp.where(positive >= 0.0, e_own, 1.0) / (1.0 + e_own)
    own_loss = jnp.maximum(-positive, 0.0) + log1p_sum(e_own)
    own_weight[...] = jnp.broadcast_to(own_c.astype(BF16).astype(F32), (N, 128))
    first = lax.broadcasted_iota(jnp.int32, (8, 2 * N), 0) + lax.broadcasted_iota(jnp.int32, (8, 2 * N), 1) == 0
    sums[0] = jnp.where(first, jnp.sum(own_loss), 0.0)
    sums[1] = jnp.where(first, jnp.sum(own_c), 0.0)
    tt[3, :, 0:N] = tbuf[3, 0:N].T

    def hop(k):
        right[k].wait_recv()
        left[k].wait_recv()
        if k + 2 < 7:
            start(right[k + 2], left[k + 2])

    def logits(p, q):
        return jnp.dot(ibuf[pl.ds(2 * p, 2)].reshape(4 * N, W), tt[q], preferred_element_type=F32)

    def weights(dots, masked):
        u = dots * scale + shift[masked]
        e = jnp.exp2(-jnp.abs(u))
        d = 1.0 + e
        inv = pl.reciprocal(d, approx=True)
        inv = inv * (2.0 - d * inv)
        c = jnp.where(u >= 0.0, 1.0, e) * inv
        cb = c.astype(BF16)
        cbuf[...] = cb
        ctbuf[...] = cb.T
        parts = [e[8 * i : 8 * i + 8] for i in range(4 * N // 8)]
        while len(parts) > 1:
            parts = [a + (h + a * h) for a, h in zip(parts[::2], parts[1::2])]
        tail = log1p_sum(parts[0])
        linear = jnp.sum(jnp.maximum(u, 0.0).reshape(4 * N // 8, 8, 2 * N), axis=0)
        csum = jnp.sum(c.reshape(4 * N // 8, 8, 2 * N), axis=0)
        sums[0] += tail + linear * LN2
        sums[1] += csum

    def grads(p, q):
        c, ct = cbuf[...], ctbuf[...]
        for lo, hi in ((0, W),):
            g_i[pl.ds(2 * p, 2), :, lo:hi] += jnp.dot(c, tbuf[q, :, lo:hi], preferred_element_type=F32).reshape(2, 2 * N, hi - lo)
            g_t[q, :, lo:hi] += jnp.dot(
                ct, ibuf[pl.ds(2 * p, 2), :, lo:hi].reshape(4 * N, hi - lo), preferred_element_type=F32
            )

    def text_part(name, half):
        q, at = T_PLACE[name]
        return g_t[q, at * N + half * H : at * N + half * H + H]

    def ring_back(k):
        name = 4 - (k + 1) // 2
        for sign, send, recv, out in (("R", zl_send, zl_recv, back_left), ("L", zr_send, zr_recv, back_right)):
            half = (k % 2) if sign == "R" else 1 - (k % 2)
            share = text_part(f"{sign}{name}", half)
            if k >= 2:
                out[k - 2].wait_recv()
                share = share + recv[k - 2].astype(F32)
            send[k] = share.astype(BF16)
            start(out[k])

    def shared(b, lo, hi):
        return g_i[b, lo:hi] + tw_recv[b, lo:hi].astype(F32)

    def leave_second():
        back_twin[7].wait_recv()
        sf_send[0, 0:SIDE_A] = shared(7, A, C).astype(BF16)
        sf_send[1, 0 : SIDE - SIDE_A] = shared(7, C, N).astype(BF16)
        start(*back_side2)
        pt_send[2, 0:A] = shared(7, 0, A).astype(BF16)
        start(back_across[2])

    def to_twin(b):
        tw_send[b] = g_i[b, N : 2 * N].astype(BF16)
        start(back_twin[b])

    def swapped(i):
        swap[i].wait_recv()
        start_if(y < 3, direct[1][i])
        start_if(y == 0, direct[3][i])

    def arrived(i):
        for r in (1, 3):
            direct[r][i].wait_recv()
        if i == 0:
            start(across[1][0], across[3][0], direct2[0])
        else:
            start(direct2[1], twins[P_SLOT[1]], twins[P_SLOT[3]])

    swapped(0)
    across[0][0].wait_recv()
    start(side_swap)
    start_if(y > 0, side[3])
    start_if(y == 3, side[1])
    hop(0)
    swapped(1)
    hop(1)
    side_swap.wait_recv()
    start_if(y < 3, side[1])
    start_if(y == 0, side[3])
    across[0][1].wait_recv()
    start(twins[S_SLOT[0]])
    arrived(0)
    tt[0] = tbuf[0].T
    twins[0].wait_recv()
    twins[1].wait_recv()

    def step(n, carry):
        @pl.when(n == 1)
        def _():
            hop(2)
            arrived(1)
            side[1].wait_recv()
            side[3].wait_recv()
            start(*side2)
            hop(3)
            direct2[0].wait_recv()
            start(across[2][0])
            twins[2].wait_recv()
            twins[3].wait_recv()

        @pl.when(n == 2)
        def _():
            across[1][0].wait_recv()
            across[3][0].wait_recv()
            start(twins[S_SLOT[1]], twins[S_SLOT[3]])
            tt[1] = tbuf[1].T

        @pl.when(n == 3)
        def _():
            hop(4)

        @pl.when(n == 4)
        def _():
            direct2[1].wait_recv()
            start(twins[P_SLOT[2]])
            twins[4].wait_recv()
            twins[5].wait_recv()

        @pl.when(n == 6)
        def _():
            hop(5)
            tt[2] = tbuf[2].T

        @pl.when(n == 7)
        def _():
            side2[0].wait_recv()
            side2[1].wait_recv()
            across[2][0].wait_recv()
            start(twins[S_SLOT[2]])

        @pl.when(n == 9)
        def _():
            twins[6].wait_recv()
            twins[7].wait_recv()

        @pl.when(n == 12)
        def _():
            hop(6)
            tt[3, :, N : 2 * N] = tbuf[3, N : 2 * N].T

        @pl.when(n == 13)
        def _():
            for c in started:
                c.wait_send()
            started.clear()
            ring_back(1)

        @pl.when(n == 14)
        def _():
            to_twin(7)
            to_twin(6)

        @pl.when(n == 15)
        def _():
            to_twin(4)
            to_twin(5)

        p, q = unit_of(n)
        before_p, before_q = unit_of(n - 1)
        dots = logits(p, q)
        grads(before_p, before_q)
        weights(dots, jnp.where(n == 15, 1, 0))
        return carry

    weights(logits(0, 0), 0)
    lax.fori_loop(1, 16, step, 0)
    grads(0, 3)

    def home(r, lo, hi):
        crossed = N if r == 0 else A
        if hi <= crossed:
            return shared(P_SLOT[r], lo, hi) + pt_recv[r, lo:hi].astype(F32)
        if lo >= crossed:
            return shared(P_SLOT[r], lo, hi)
        return jnp.concatenate([home(r, lo, crossed), home(r, crossed, hi)], axis=0)

    def keep(where, values):
        return jnp.where(where, values.astype(F32), 0.0)

    ring_back(0)
    for b in (2, 3, 1, 0):
        to_twin(b)
    l1[0, 0:8] = sums[0, :, 0:128] + sums[0, :, 128:256]
    l1[0, 8:16] = sums[1, :, 0:128] + sums[1, :, 128:256]
    start(loss_twin)
    ring_back(3)

    leave_second()
    for r in (1, 3, 0):
        back_twin[S_SLOT[r]].wait_recv()
        pt_send[r, 0:A] = shared(S_SLOT[r], 0, A).astype(BF16)
        start(back_across[r])
    ring_back(2)

    for i, r in ((0, 1), (1, 3)):
        b = S_SLOT[r]
        plain, joined = (slice(C, N), slice(A, C)) if i == 0 else (slice(A, C), slice(C, N))
        sx_send[i, plain.start - A : plain.stop - A] = shared(b, plain.start, plain.stop).astype(BF16)
        back_side2[i].wait_recv()
        sx_send[i, joined.start - A : joined.stop - A] = (shared(b, joined.start, joined.stop) + sf_recv[i].astype(F32)).astype(BF16)
        start(back_side[r])
    back_twin[P_SLOT[2]].wait_recv()
    back_across[2].wait_recv()
    f_send[0] = home(2, 0, H).astype(BF16)
    f_send[1] = home(2, H, N).astype(BF16)
    start(*back_direct2)
    loss_twin.wait_recv()
    l2[z] = l1[0] + l1[1]
    start(*loss_ring)
    ring_back(5)
    for r in (1, 3):
        back_side[r].wait_recv()
    xs_send[...] = (keep(y < 3, sx_recv[0]) + keep(y == 0, sx_recv[1])).astype(BF16)
    start(back_side_swap)

    def send_home(r):
        i = r // 2
        back_twin[P_SLOT[r]].wait_recv()
        back_across[r].wait_recv()
        for k in (1 - i, i):
            lo, hi = halves[k]
            share = home(r, lo, hi)
            if k == i:
                back_direct2[i].wait_recv()
                share = share + f_recv[i].astype(F32)
            dr_send[i, lo:hi] = share.astype(BF16)
            start(back_direct[r][k])

    ring_back(4)
    send_home(1)
    send_home(3)
    back_side_swap.wait_recv()
    side_sum = keep(y == 3, sx_recv[0]) + keep(y > 0, sx_recv[1]) + xs_recv[...].astype(F32)
    pt_send[0, A:N] = (shared(1, A, N) + side_sum).astype(BF16)
    start(back_across_rest)
    for c in loss_ring:
        c.wait_recv()
    l3[x] = sum([l2[k] for k in range(1, 8)], l2[0])
    start(*loss_row)

    def swap_home(k):
        lo, hi = halves[k]
        back_direct[1][k].wait_recv()

        @pl.when(y == 0)
        def _():
            back_direct[3][k].wait_recv()
            xa_send[lo:hi] = (dr_recv[0, lo:hi].astype(F32) + dr_recv[1, lo:hi].astype(F32)).astype(BF16)

        @pl.when(y > 0)
        def _():
            xa_send[lo:hi] = keep(y < 3, dr_recv[0, lo:hi]).astype(BF16)

        start(back_swap[k])

    swap_home(1)
    ring_back(6)
    swap_home(0)
    for c in loss_row:
        c.wait_recv()
    l4[y] = sum([l3[k] for k in range(1, 4)], l3[0])
    start(*loss_col)
    x_unit, x_inverse = unit_rows(images)
    y_unit, y_inverse = unit_rows(texts)
    own_cb = own_weight[:, 0:1]
    for half in (1, 0):
        rows = slice(half * H, half * H + H)
        back_left[6 - half].wait_recv()
        back_right[5 + half].wait_recv()
        came = zl_recv[6 - half].astype(F32) + zr_recv[5 + half].astype(F32)
        gy = temp * (g_t[3, rows] + came + own_cb[rows] * ibuf[0, rows].astype(F32))
        yu = y_unit[rows]
        text_grad[rows] = (gy - yu * jnp.sum(yu * gy, axis=-1, keepdims=True)) * y_inverse[rows]

    back_twin[0].wait_recv()
    back_across[0].wait_recv()
    back_across_rest.wait_recv()
    for k, (lo, hi) in enumerate(halves):
        back_swap[k].wait_recv()
        pl.when(y > 0)(back_direct[3][k].wait_recv)
        came = keep(y == 3, dr_recv[0, lo:hi]) + keep(y > 0, dr_recv[1, lo:hi]) + xa_recv[lo:hi].astype(F32)
        gx = temp * (home(0, lo, hi) + own_cb[lo:hi] * tbuf[3, lo:hi].astype(F32) + came)
        xu = x_unit[lo:hi]
        image_grad[lo:hi] = (gx - xu * jnp.sum(xu * gx, axis=-1, keepdims=True)) * x_inverse[lo:hi]

    for c in loss_col:
        c.wait_recv()
    total = sum([l4[k] for k in range(1, 4)], l4[0])
    pairs = N * 256
    loss_out[...] = jnp.full((1,), jnp.sum(total[0:8]) / pairs, F32)
    bias_out[...] = jnp.full((1,), jnp.sum(total[8:16]) / pairs, F32)

    for c in started:
        c.wait_send()


def per_device(images, texts, log_temp, bias):
    N, W = images.shape
    H = N // 2
    vmem = pl.BlockSpec(memory_space=pltpu.VMEM)
    smem = pl.BlockSpec(memory_space=pltpu.SMEM)
    scratch = [
        pltpu.VMEM((10, 2 * N, W), BF16),
        pltpu.VMEM((4, 2 * N, W), BF16),
        pltpu.VMEM((4, W, 2 * N), BF16),
        pltpu.VMEM((8, 2 * N, W), F32),
        pltpu.VMEM((4, 2 * N, W), F32),
        pltpu.VMEM((4 * N, 2 * N), BF16),
        pltpu.VMEM((2 * N, 4 * N), BF16),
        pltpu.VMEM((2, 4 * N, 2 * N), F32),
        pltpu.VMEM((2, 8, 2 * N), F32),
        pltpu.VMEM((N, 128), F32),
        *[pltpu.VMEM((8, N, W), BF16)] * 2,
        *[pltpu.VMEM((4, N, W), BF16)] * 2,
        *[pltpu.VMEM((2, N, W), BF16)] * 2,
        *[pltpu.VMEM((N, W), BF16)] * 2,
        *[pltpu.VMEM((2, H, W), BF16)] * 2,
        *[pltpu.VMEM((2, SIDE, W), BF16)] * 2,
        *[pltpu.VMEM((SIDE, W), BF16)] * 2,
        *[pltpu.VMEM((2, SIDE_A, W), BF16)] * 2,
        *[pltpu.VMEM((7, H, W), BF16)] * 4,
        pltpu.VMEM((2, 16, 128), F32),
        pltpu.VMEM((8, 16, 128), F32),
        pltpu.VMEM((4, 16, 128), F32),
        pltpu.VMEM((4, 16, 128), F32),
        pltpu.SemaphoreType.DMA((SEND_SEMAPHORES,)),
        pltpu.SemaphoreType.DMA((MESSAGES,)),
    ]
    return pl.pallas_call(
        kernel,
        out_shape=(
            jax.ShapeDtypeStruct((N, W), F32),
            jax.ShapeDtypeStruct((N, W), F32),
            jax.ShapeDtypeStruct((1,), F32),
            jax.ShapeDtypeStruct((1,), F32),
        ),
        in_specs=[vmem, vmem, smem, smem],
        out_specs=(vmem, vmem, vmem, vmem),
        scratch_shapes=scratch,
        compiler_params=pltpu.CompilerParams(
            collective_id=0, has_side_effects=True, vmem_limit_bytes=46 * 1024 * 1024
        ),
    )(images, texts, log_temp, bias)


def solution(mesh):
    placed = (P(("grp", "mem"), None), P(("grp", "mem"), None), P(), P())
    return jax.shard_map(
        per_device,
        mesh=mesh,
        in_specs=placed,
        out_specs=(P(("grp", "mem"), None), P(("grp", "mem"), None), P(), P()),
        check_vma=False,
    )
```

```python
import functools
import math

import jax
import jax.numpy as jnp
from jax import lax
from jax.experimental import pallas as pl
from jax.experimental.pallas import tpu as pltpu
from jax.sharding import PartitionSpec as P

MESH = pl.DeviceIdType.MESH
F32 = jnp.float32
BF16 = jnp.bfloat16
LOG2E = math.log2(math.e)
LN2 = math.log(2.0)
SIDE = 64
SIDE_A = 32
MESSAGES_OUT = 40
MESSAGES = 93
SEND_SEMAPHORES = MESSAGES - MESSAGES_OUT


P_SLOT = {0: 0, 1: 2, 3: 3, 2: 6}
S_SLOT = {0: 1, 1: 4, 3: 5, 2: 7}
T_PLACE = {"R1": (0, 0), "L1": (0, 1), "R2": (1, 0), "L2": (1, 1), "R3": (2, 0), "L3": (2, 1), "R0": (3, 0), "L0": (3, 0), "R4": (3, 1), "L4": (3, 1)}


UNITS = (
    (0, 0), (1, 0), (0, 1), (1, 1), (2, 0), (2, 1), (0, 2), (1, 2),
    (2, 2), (3, 0), (3, 1), (3, 2), (3, 3), (2, 3), (1, 3), (0, 3),
)


def unit_of(n):
    p, q = UNITS[0]
    for k in range(1, len(UNITS)):
        p = jnp.where(n == k, UNITS[k][0], p)
        q = jnp.where(n == k, UNITS[k][1], q)
    return p, q


def log1p_sum(q):
    series = q * (1.0 - q * (0.5 - q * (1.0 / 3.0 - q * 0.25)))
    return jnp.where(q < 0.0078125, series, jnp.log(1.0 + q))


def kernel(
    images, texts, log_temp, bias,
    image_grad, text_grad, loss_out, bias_out,
    ibuf, tbuf, tt, g_i, g_t, cbuf, ctbuf, shift, sums, own_weight,
    tw_send, tw_recv, pt_send, pt_recv, dr_send, dr_recv, xa_send, xa_recv, f_send, f_recv,
    sx_send, sx_recv, xs_send, xs_recv, sf_send, sf_recv,
    zl_send, zl_recv, zr_send, zr_recv,
    l1, l2, l3, l4, ssem, rsem,
):
    N, W = images.shape
    H = N // 2
    A = N - SIDE
    C = A + SIDE_A
    g = lax.axis_index("grp")
    m = lax.axis_index("mem")
    y = lax.rem(g, 4)
    xh = lax.div(g, 4)
    xl = lax.div(m, 16)
    z = lax.rem(lax.div(m, 2), 8)
    core = lax.rem(m, 2)
    x = xh * 2 + xl

    def dev(x_hi, yy, x_lo, zz, cc):
        return (x_hi * 4 + lax.rem(yy, 4), x_lo * 16 + lax.rem(zz, 8) * 2 + cc)

    twin = dev(xh, y, xl, z, 1 - core)
    ring = [dev(xh, y, xl, z + k, core) for k in range(8)]
    ahead, back = ring[1], ring[7]
    partner = dev(xh, y, 1 - xl, z, core)
    adjacent = dev(1 - xh, y, 1 - xl, z, core)
    far = dev(1 - xh, y, xl, z, core)
    north, across_y, south = (dev(xh, y + k, xl, z, core) for k in (1, 2, 3))
    up = dev(jnp.where(y == 3, 1 - xh, xh), y + 1, jnp.where(y == 3, 1 - xl, xl), z, core)
    down = dev(jnp.where(y == 0, 1 - xh, xh), y + 3, jnp.where(y == 0, 1 - xl, xl), z, core)

    count = [0]
    started = []

    def message(src, dst, device):
        i = count[0]
        count[0] += 1
        return pltpu.make_async_remote_copy(
            src_ref=src, dst_ref=dst, send_sem=ssem.at[i if i < MESSAGES_OUT else i - MESSAGES_OUT], recv_sem=rsem.at[i],
            device_id=device, device_id_type=MESH,
        )

    def start(*copies):
        for c in copies:
            c.start()
            started.append(c)

    def start_if(where, *copies):
        for c in copies:
            pl.when(where)(c.start)

    def place(name, half):
        q, at = T_PLACE[name]
        return tbuf.at[q, pl.ds(at * N + half * H, H)]

    right, left = [], []
    for k in range(7):
        a, b_ = k // 2, k // 2 + 1
        right.append(message(place(f"R{a}", k % 2), place(f"R{b_}", k % 2), ahead))
        left.append(message(place(f"L{a}", 1 - k % 2), place(f"L{b_}", 1 - k % 2), back))

    def rows_of(b, lo, hi):
        return ibuf.at[b, pl.ds(lo, hi - lo)]

    def move(src, dst, lo, hi, device):
        return message(rows_of(src, lo, hi), rows_of(dst, lo, hi), device)

    halves = ((0, H), (H, N))
    go_north, go_south = jnp.where(y < 3, 8, 0), jnp.where(y == 0, 8, 0)
    swap = [move(0, 8, lo, hi, adjacent) for lo, hi in halves]
    direct = {1: [move(go_north, P_SLOT[1], lo, hi, north) for lo, hi in halves], 3: [move(go_south, P_SLOT[3], lo, hi, south) for lo, hi in halves]}

    direct2 = [move(P_SLOT[1], P_SLOT[2], 0, H, up), move(P_SLOT[3], P_SLOT[2], H, N, down)]
    across = {0: [move(0, S_SLOT[0], lo, hi, partner) for lo, hi in ((A, N), (0, A))]}
    for r in (1, 3, 2):
        across[r] = [move(P_SLOT[r], S_SLOT[r], 0, A, partner)]
    side_swap = move(S_SLOT[0], 9, A, N, adjacent)
    side = {
        1: move(jnp.where(y < 3, 9, S_SLOT[0]), S_SLOT[1], A, N, north),
        3: move(jnp.where(y == 0, 9, S_SLOT[0]), S_SLOT[3], A, N, south),
    }
    side2 = [move(S_SLOT[1], S_SLOT[2], A, C, up), move(S_SLOT[3], S_SLOT[2], C, N, down)]
    twins = [message(rows_of(b, 0, N), rows_of(b, N, 2 * N), twin) for b in range(8)]

    assert count[0] == MESSAGES_OUT
    back_twin = [message(tw_send.at[b], tw_recv.at[b], twin) for b in range(8)]
    back_across = {
        r: message(pt_send.at[r, pl.ds(0, N if r == 0 else A)], pt_recv.at[r, pl.ds(0, N if r == 0 else A)], partner)
        for r in range(4)
    }
    back_direct = {
        r: [message(dr_send.at[i, pl.ds(lo, H)], dr_recv.at[i, pl.ds(lo, H)], d) for lo in (0, H)]
        for i, r, d in ((0, 1, south), (1, 3, north))
    }
    back_swap = [message(xa_send.at[pl.ds(lo, H)], xa_recv.at[pl.ds(lo, H)], adjacent) for lo in (0, H)]
    back_side = {r: message(sx_send.at[i], sx_recv.at[i], d) for i, r, d in ((0, 1, south), (1, 3, north))}
    back_side_swap = message(xs_send, xs_recv, adjacent)

    back_direct2 = [message(f_send.at[i], f_recv.at[i], d) for i, d in ((0, down), (1, up))]
    back_side2 = [message(sf_send.at[i], sf_recv.at[i], d) for i, d in ((0, down), (1, up))]
    back_left = [message(zl_send.at[k], zl_recv.at[k], back) for k in range(7)]
    back_right = [message(zr_send.at[k], zr_recv.at[k], ahead) for k in range(7)]
    loss_twin = message(l1.at[0], l1.at[1], twin)
    loss_ring = [message(l2.at[z], l2.at[z], ring[k]) for k in range(1, 8)]
    loss_row = [message(l3.at[x], l3.at[x], d) for d in (partner, adjacent, far)]
    loss_col = [message(l4.at[y], l4.at[y], d) for d in (north, across_y, south)]

    far_north, far_south = dev(1 - xh, y + 1, 1 - xl, z, core), dev(1 - xh, y + 3, 1 - xl, z, core)

    peers = [twin, *ring[1:], partner, adjacent, far, north, across_y, south, far_north, far_south]
    barrier = pltpu.get_barrier_semaphore()
    for p in peers:
        pl.semaphore_signal(barrier, inc=1, device_id=p, device_id_type=MESH)

    def unit_rows(ref):
        full = ref[...].astype(F32)
        inverse = lax.rsqrt(jnp.sum(full * full, axis=-1, keepdims=True) + 1e-06)
        return full * inverse, inverse

    ibuf[0, 0:N] = unit_rows(images)[0].astype(BF16)
    pl.semaphore_wait(barrier, len(peers))
    start(swap[0], across[0][0])
    start_if(y > 0, direct[3][0])
    start_if(y == 3, direct[1][0])
    tbuf[3, 0:N] = unit_rows(texts)[0].astype(BF16)
    start(right[0], left[0], swap[1], across[0][1], right[1], left[1])
    start_if(y > 0, direct[3][1])
    start_if(y == 3, direct[1][1])
    start(twins[0])
    started.extend(direct[1] + direct[3] + list(side.values()))

    temp = jnp.max(jnp.exp(jnp.full((8, 128), log_temp[0], F32)))
    offset = bias[0]
    scale = temp * LOG2E
    offset2 = offset * LOG2E
    row = lax.broadcasted_iota(jnp.int32, (4 * N, 2 * N), 0)
    col = lax.broadcasted_iota(jnp.int32, (4 * N, 2 * N), 1)
    shift[0] = jnp.full((4 * N, 2 * N), offset2, F32)
    shift[1] = jnp.where((row == col) & (row < N), -1e30, offset2)

    def clear(i, carry):
        zeros = jnp.zeros((32, W), F32)
        g_i[lax.div(i, 8), pl.ds(pl.multiple_of(lax.rem(i, 8) * 32, 32), 32)] = zeros

        @pl.when(i < 32)
        def _():
            g_t[lax.div(i, 8), pl.ds(pl.multiple_of(lax.rem(i, 8) * 32, 32), 32)] = zeros

        return carry

    lax.fori_loop(0, 64, clear, 0)

    positive = temp * jnp.sum(ibuf[0, 0:N].astype(F32) * tbuf[3, 0:N].astype(F32), axis=-1, keepdims=True) + offset
    e_own = jnp.exp(-jnp.abs(positive))
    own_c = -jnp.where(positive >= 0.0, e_own, 1.0) / (1.0 + e_own)
    own_loss = jnp.maximum(-positive, 0.0) + log1p_sum(e_own)
    own_weight[...] = jnp.broadcast_to(own_c.astype(BF16).astype(F32), (N, 128))
    first = lax.broadcasted_iota(jnp.int32, (8, 2 * N), 0) + lax.broadcasted_iota(jnp.int32, (8, 2 * N), 1) == 0
    sums[0] = jnp.where(first, jnp.sum(own_loss), 0.0)
    sums[1] = jnp.where(first, jnp.sum(own_c), 0.0)
    tt[3, :, 0:N] = tbuf[3, 0:N].T

    def hop(k):
        right[k].wait_recv()
        left[k].wait_recv()
        if k + 2 < 7:
            start(right[k + 2], left[k + 2])

    def logits(p, q):
        return jnp.dot(ibuf[pl.ds(2 * p, 2)].reshape(4 * N, W), tt[q], preferred_element_type=F32)

    def weights(dots, masked):
        u = dots * scale + shift[masked]
        e = jnp.exp2(-jnp.abs(u))
        d = 1.0 + e
        inv = pl.reciprocal(d, approx=True)
        inv = inv * (2.0 - d * inv)
        c = jnp.where(u >= 0.0, 1.0, e) * inv
        cb = c.astype(BF16)
        cbuf[...] = cb
        ctbuf[...] = cb.T
        parts = [e[8 * i : 8 * i + 8] for i in range(4 * N // 8)]
        while len(parts) > 1:
            parts = [a + (h + a * h) for a, h in zip(parts[::2], parts[1::2])]
        tail = log1p_sum(parts[0])
        linear = jnp.sum(jnp.maximum(u, 0.0).reshape(4 * N // 8, 8, 2 * N), axis=0)
        csum = jnp.sum(c.reshape(4 * N // 8, 8, 2 * N), axis=0)
        sums[0] += tail + linear * LN2
        sums[1] += csum

    def grads(p, q):
        c, ct = cbuf[...], ctbuf[...]
        for lo, hi in ((0, W),):
            g_i[pl.ds(2 * p, 2), :, lo:hi] += jnp.dot(c, tbuf[q, :, lo:hi], preferred_element_type=F32).reshape(2, 2 * N, hi - lo)
            g_t[q, :, lo:hi] += jnp.dot(
                ct, ibuf[pl.ds(2 * p, 2), :, lo:hi].reshape(4 * N, hi - lo), preferred_element_type=F32
            )

    def text_part(name, half):
        q, at = T_PLACE[name]
        return g_t[q, at * N + half * H : at * N + half * H + H]

    def ring_back(k):
        name = 4 - (k + 1) // 2
        for sign, send, recv, out in (("R", zl_send, zl_recv, back_left), ("L", zr_send, zr_recv, back_right)):
            half = (k % 2) if sign == "R" else 1 - (k % 2)
            share = text_part(f"{sign}{name}", half)
            if k >= 2:
                out[k - 2].wait_recv()
                share = share + recv[k - 2].astype(F32)
            send[k] = share.astype(BF16)
            start(out[k])

    def shared(b, lo, hi):
        return g_i[b, lo:hi] + tw_recv[b, lo:hi].astype(F32)

    def leave_second():
        back_twin[7].wait_recv()
        sf_send[0, 0:SIDE_A] = shared(7, A, C).astype(BF16)
        sf_send[1, 0 : SIDE - SIDE_A] = shared(7, C, N).astype(BF16)
        start(*back_side2)
        pt_send[2, 0:A] = shared(7, 0, A).astype(BF16)
        start(back_across[2])

    def to_twin(b):
        tw_send[b] = g_i[b, N : 2 * N].astype(BF16)
        start(back_twin[b])

    def swapped(i):
        swap[i].wait_recv()
        start_if(y < 3, direct[1][i])
        start_if(y == 0, direct[3][i])

    def arrived(i):
        for r in (1, 3):
            direct[r][i].wait_recv()
        if i == 0:
            start(across[1][0], across[3][0], direct2[0])
        else:
            start(direct2[1], twins[P_SLOT[1]], twins[P_SLOT[3]])

    swapped(0)
    across[0][0].wait_recv()
    start(side_swap)
    start_if(y > 0, side[3])
    start_if(y == 3, side[1])
    hop(0)
    swapped(1)
    hop(1)
    side_swap.wait_recv()
    start_if(y < 3, side[1])
    start_if(y == 0, side[3])
    across[0][1].wait_recv()
    start(twins[S_SLOT[0]])
    arrived(0)
    tt[0] = tbuf[0].T
    twins[0].wait_recv()
    twins[1].wait_recv()

    def step(n, carry):
        @pl.when(n == 1)
        def _():
            arrived(1)
            hop(2)
            side[1].wait_recv()
            side[3].wait_recv()
            start(*side2)
            twins[2].wait_recv()
            twins[3].wait_recv()

        @pl.when(n == 2)
        def _():
            direct2[0].wait_recv()
            start(across[2][0])
            hop(3)
            across[1][0].wait_recv()
            across[3][0].wait_recv()
            start(twins[S_SLOT[1]], twins[S_SLOT[3]])
            tt[1] = tbuf[1].T

        @pl.when(n == 4)
        def _():
            direct2[1].wait_recv()
            start(twins[P_SLOT[2]])
            hop(4)
            twins[4].wait_recv()
            twins[5].wait_recv()

        @pl.when(n == 6)
        def _():
            side2[0].wait_recv()
            side2[1].wait_recv()
            across[2][0].wait_recv()
            start(twins[S_SLOT[2]])
            hop(5)
            tt[2] = tbuf[2].T

        @pl.when(n == 9)
        def _():
            twins[6].wait_recv()
            twins[7].wait_recv()

        @pl.when(n == 12)
        def _():
            hop(6)
            tt[3, :, N : 2 * N] = tbuf[3, N : 2 * N].T

        @pl.when(n == 13)
        def _():
            for c in started:
                c.wait_send()
            started.clear()
            ring_back(1)

        @pl.when(n == 14)
        def _():
            to_twin(7)
            to_twin(6)

        @pl.when(n == 15)
        def _():
            to_twin(4)
            to_twin(5)

        p, q = unit_of(n)
        before_p, before_q = unit_of(n - 1)
        dots = logits(p, q)
        grads(before_p, before_q)
        weights(dots, jnp.where(n == 15, 1, 0))
        return carry

    weights(logits(0, 0), 0)
    lax.fori_loop(1, 16, step, 0)
    grads(0, 3)

    def home(r, lo, hi):
        crossed = N if r == 0 else A
        if hi <= crossed:
            return shared(P_SLOT[r], lo, hi) + pt_recv[r, lo:hi].astype(F32)
        if lo >= crossed:
            return shared(P_SLOT[r], lo, hi)
        return jnp.concatenate([home(r, lo, crossed), home(r, crossed, hi)], axis=0)

    def keep(where, values):
        return jnp.where(where, values.astype(F32), 0.0)

    ring_back(0)
    for b in (2, 3, 1, 0):
        to_twin(b)
    l1[0, 0:8] = sums[0, :, 0:128] + sums[0, :, 128:256]
    l1[0, 8:16] = sums[1, :, 0:128] + sums[1, :, 128:256]
    start(loss_twin)

    leave_second()
    for r in (1, 3):
        back_twin[S_SLOT[r]].wait_recv()
        pt_send[r, 0:A] = shared(S_SLOT[r], 0, A).astype(BF16)
        start(back_across[r])
    ring_back(2)

    for i, r in ((0, 1), (1, 3)):
        b = S_SLOT[r]
        plain, joined = (slice(C, N), slice(A, C)) if i == 0 else (slice(A, C), slice(C, N))
        sx_send[i, plain.start - A : plain.stop - A] = shared(b, plain.start, plain.stop).astype(BF16)
        back_side2[i].wait_recv()
        sx_send[i, joined.start - A : joined.stop - A] = (shared(b, joined.start, joined.stop) + sf_recv[i].astype(F32)).astype(BF16)
        start(back_side[r])
    back_twin[P_SLOT[2]].wait_recv()
    back_across[2].wait_recv()
    f_send[0] = home(2, 0, H).astype(BF16)
    f_send[1] = home(2, H, N).astype(BF16)
    start(*back_direct2)
    loss_twin.wait_recv()
    l2[z] = l1[0] + l1[1]
    start(*loss_ring)
    ring_back(3)
    for r in (1, 3):
        back_side[r].wait_recv()
    xs_send[...] = (keep(y < 3, sx_recv[0]) + keep(y == 0, sx_recv[1])).astype(BF16)
    start(back_side_swap)

    def send_home(r):
        i = r // 2
        back_twin[P_SLOT[r]].wait_recv()
        back_across[r].wait_recv()
        for k in (1 - i, i):
            lo, hi = halves[k]
            share = home(r, lo, hi)
            if k == i:
                back_direct2[i].wait_recv()
                share = share + f_recv[i].astype(F32)
            dr_send[i, lo:hi] = share.astype(BF16)
            start(back_direct[r][k])

    send_home(1)
    ring_back(4)
    send_home(3)
    for c in loss_ring:
        c.wait_recv()
    l3[x] = sum([l2[k] for k in range(1, 8)], l2[0])
    start(*loss_row)
    back_twin[1].wait_recv()
    back_side_swap.wait_recv()
    pt_send[0, 0:A] = shared(1, 0, A).astype(BF16)
    side_sum = keep(y == 3, sx_recv[0]) + keep(y > 0, sx_recv[1]) + xs_recv[...].astype(F32)
    pt_send[0, A:N] = (shared(1, A, N) + side_sum).astype(BF16)
    start(back_across[0])
    ring_back(5)

    def swap_home(k):
        lo, hi = halves[k]
        back_direct[1][k].wait_recv()

        @pl.when(y == 0)
        def _():
            back_direct[3][k].wait_recv()
            xa_send[lo:hi] = (dr_recv[0, lo:hi].astype(F32) + dr_recv[1, lo:hi].astype(F32)).astype(BF16)

        @pl.when(y > 0)
        def _():
            xa_send[lo:hi] = keep(y < 3, dr_recv[0, lo:hi]).astype(BF16)

        start(back_swap[k])

    swap_home(0)
    ring_back(6)
    swap_home(1)
    for c in loss_row:
        c.wait_recv()
    l4[y] = sum([l3[k] for k in range(1, 4)], l3[0])
    start(*loss_col)
    x_unit, x_inverse = unit_rows(images)
    y_unit, y_inverse = unit_rows(texts)
    own_cb = own_weight[:, 0:1]
    for half in (1, 0):
        rows = slice(half * H, half * H + H)
        back_left[6 - half].wait_recv()
        back_right[5 + half].wait_recv()
        came = zl_recv[6 - half].astype(F32) + zr_recv[5 + half].astype(F32)
        gy = temp * (g_t[3, rows] + came + own_cb[rows] * ibuf[0, rows].astype(F32))
        yu = y_unit[rows]
        text_grad[rows] = (gy - yu * jnp.sum(yu * gy, axis=-1, keepdims=True)) * y_inverse[rows]

    back_twin[0].wait_recv()
    back_across[0].wait_recv()
    for k, (lo, hi) in enumerate(halves):
        back_swap[k].wait_recv()
        pl.when(y > 0)(back_direct[3][k].wait_recv)
        came = keep(y == 3, dr_recv[0, lo:hi]) + keep(y > 0, dr_recv[1, lo:hi]) + xa_recv[lo:hi].astype(F32)
        gx = temp * (home(0, lo, hi) + own_cb[lo:hi] * tbuf[3, lo:hi].astype(F32) + came)
        xu = x_unit[lo:hi]
        image_grad[lo:hi] = (gx - xu * jnp.sum(xu * gx, axis=-1, keepdims=True)) * x_inverse[lo:hi]

    for c in loss_col:
        c.wait_recv()
    total = sum([l4[k] for k in range(1, 4)], l4[0])
    pairs = N * 256
    loss_out[...] = jnp.full((1,), jnp.sum(total[0:8]) / pairs, F32)
    bias_out[...] = jnp.full((1,), jnp.sum(total[8:16]) / pairs, F32)

    for c in started:
        c.wait_send()


def per_device(images, texts, log_temp, bias):
    N, W = images.shape
    H = N // 2
    vmem = pl.BlockSpec(memory_space=pltpu.VMEM)
    smem = pl.BlockSpec(memory_space=pltpu.SMEM)
    scratch = [
        pltpu.VMEM((10, 2 * N, W), BF16),
        pltpu.VMEM((4, 2 * N, W), BF16),
        pltpu.VMEM((4, W, 2 * N), BF16),
        pltpu.VMEM((8, 2 * N, W), F32),
        pltpu.VMEM((4, 2 * N, W), F32),
        pltpu.VMEM((4 * N, 2 * N), BF16),
        pltpu.VMEM((2 * N, 4 * N), BF16),
        pltpu.VMEM((2, 4 * N, 2 * N), F32),
        pltpu.VMEM((2, 8, 2 * N), F32),
        pltpu.VMEM((N, 128), F32),
        *[pltpu.VMEM((8, N, W), BF16)] * 2,
        *[pltpu.VMEM((4, N, W), BF16)] * 2,
        *[pltpu.VMEM((2, N, W), BF16)] * 2,
        *[pltpu.VMEM((N, W), BF16)] * 2,
        *[pltpu.VMEM((2, H, W), BF16)] * 2,
        *[pltpu.VMEM((2, SIDE, W), BF16)] * 2,
        *[pltpu.VMEM((SIDE, W), BF16)] * 2,
        *[pltpu.VMEM((2, SIDE_A, W), BF16)] * 2,
        *[pltpu.VMEM((7, H, W), BF16)] * 4,
        pltpu.VMEM((2, 16, 128), F32),
        pltpu.VMEM((8, 16, 128), F32),
        pltpu.VMEM((4, 16, 128), F32),
        pltpu.VMEM((4, 16, 128), F32),
        pltpu.SemaphoreType.DMA((SEND_SEMAPHORES,)),
        pltpu.SemaphoreType.DMA((MESSAGES,)),
    ]
    return pl.pallas_call(
        kernel,
        out_shape=(
            jax.ShapeDtypeStruct((N, W), F32),
            jax.ShapeDtypeStruct((N, W), F32),
            jax.ShapeDtypeStruct((1,), F32),
            jax.ShapeDtypeStruct((1,), F32),
        ),
        in_specs=[vmem, vmem, smem, smem],
        out_specs=(vmem, vmem, vmem, vmem),
        scratch_shapes=scratch,
        compiler_params=pltpu.CompilerParams(
            collective_id=0, has_side_effects=True, vmem_limit_bytes=46 * 1024 * 1024
        ),
    )(images, texts, log_temp, bias)


def solution(mesh):
    placed = (P(("grp", "mem"), None), P(("grp", "mem"), None), P(), P())
    return jax.shard_map(
        per_device,
        mesh=mesh,
        in_specs=placed,
        out_specs=(P(("grp", "mem"), None), P(("grp", "mem"), None), P(), P()),
        check_vma=False,
    )
```
